32 devices in a mesh: shard: 8 (over z, y), replica: 4 (over x, core).
Axes of the slice: x: 2, y: 2, z: 4, core: 2. Of those that a mesh axis runs over, the one named last changes fastest.
Arguments:
- grads: bfloat16 [16384, 512], P('shard'), may hold values from -1.5 to 1.5
- piece_position: int32 [32], replicated, may hold values from 0 to 31, each once
- owner: int32 [32], replicated, may hold values from 0 to 31, as said below
- stat_left: float32 [8, 4, 1, 512, 512], P('shard', 'replica'), may hold values from -1 to 8, as said below
- stat_right: float32 [8, 4, 1, 512, 512], P('shard', 'replica'), may hold values from -1 to 8, as said below
- root_left: bfloat16 [8, 4, 1, 512, 512], P('shard', 'replica'), may hold values from -1 to 4, as said below
- root_right: bfloat16 [8, 4, 1, 512, 512], P('shard', 'replica'), may hold values from -1 to 4, as said below
Outputs:
- new_left: float32 [8, 4, 1, 512, 512], P('shard', 'replica')
- new_right: float32 [8, 4, 1, 512, 512], P('shard', 'replica')
- directions: bfloat16 [16384, 512], P('shard')
The draws below stay inside these ranges and needn't reach their ends.
Inputs may be any that keep to these rules, and one draw needn't show every extreme that they name: `owner`: entries are distinct; entry v names slot v % 1 of the device with shard index (v) // the replica axis's size and replica index (v) % that size. Some device owns 1 block. `stat_left`: Symmetric; diagonal entries positive. `stat_right`: Symmetric; diagonal entries positive. `root_left`: Symmetric; diagonal entries positive. `root_right`: Symmetric; diagonal entries positive.
All inputs are finite; a program needn't handle non-finite values.
Results may differ from the reference program's by a relative error of at most 0.0049.
Values may be sent and summed in bfloat16 or wider, within the bound.
A program may use at most 64 MiB of HBM per device.

```python
import math
import jax
import jax.numpy as jnp
from jax import lax

B = 512
BLK_SH = 4
CAP = 1
NB = 32
N_SHARD = 8
N_REPLICA = 4


def symmetric_blocks(entries, diag_key, diag_low, diag_high, off_scale):
    order = entries.shape[-1]
    sym_part = (entries + jnp.swapaxes(entries, -1, -2)) * (off_scale / math.sqrt(2.0 * order))
    diag_vals = jnp.exp(jax.random.uniform(diag_key, entries.shape[:-1], jnp.float32, math.log(diag_low), math.log(diag_high)))
    identity = jnp.eye(order, dtype=jnp.float32)
    return sym_part * (1.0 - identity) + diag_vals[..., None] * identity


def slot_shape():
    return (N_SHARD, N_REPLICA, CAP, B, B)


def draw_owner(key, part):
    key = jax.random.fold_in(key, 5)
    slot_total = N_SHARD * N_REPLICA * CAP
    block_count = BLK_SH * N_SHARD
    shuffled = jax.random.permutation(key, slot_total)
    return shuffled[:block_count].astype(jnp.int32)


def stat_common(key, salt):
    key = jax.random.fold_in(key, salt)
    key_off, key_diag = jax.random.split(key)
    entries = jax.random.normal(key_off, slot_shape(), jnp.float32)
    return symmetric_blocks(entries, key_diag, 1.0, 4.0, 0.3)


def root_common(key, salt):
    key = jax.random.fold_in(key, salt)
    key_off, key_diag = jax.random.split(key)
    entries = jax.random.normal(key_off, slot_shape(), jnp.float32)
    return symmetric_blocks(entries, key_diag, 0.5, 2.0, 0.5)


def draw_stat_left(key, part):
    return stat_common(key, 7)


def draw_stat_right(key, part):
    return stat_common(key, 9)


def draw_root_left(key, part):
    return root_common(key, 11).astype(jnp.bfloat16)


def draw_root_right(key, part):
    return root_common(key, 13).astype(jnp.bfloat16)


def levels(stream_key, dims, cuts, smallest, largest):
    gain = 1.0
    for position, blocks in cuts:
        steps = jax.random.uniform(jax.random.fold_in(jax.random.fold_in(stream_key, 6), position), (blocks,), jnp.float32, smallest / len(cuts), largest / len(cuts))
        gain = gain * jnp.repeat(jnp.exp(steps), dims[position] // blocks).reshape((-1,) + (1,) * (len(dims) - 1 - position))
    return gain


def centred(rng, extent, width, reach, cuts=(), kind=jnp.bfloat16):
    result = jax.random.normal(rng, extent, jnp.float32) * width
    if len(cuts) > 0:
        result = levels(rng, extent, cuts, -0.22, 0.18) * result
    return jnp.clip(result, min=-reach, max=reach).astype(kind)


def setup_inputs(seed: int = 0) -> dict:
    key_list = jax.random.split(jax.random.key(seed), 8)
    return {
        "grads": centred(key_list[0], (NB * B, B), 0.25, 1.5, ((0, 8),)),
        "piece_position": jax.random.permutation(key_list[1], NB).astype(jnp.int32),
        "owner": draw_owner(jax.random.fold_in(key_list[7], 71), 0),
        "stat_left": draw_stat_left(jax.random.fold_in(key_list[7], 71), 0),
        "stat_right": draw_stat_right(jax.random.fold_in(key_list[7], 71), 0),
        "root_left": draw_root_left(jax.random.fold_in(key_list[7], 71), 0),
        "root_right": draw_root_right(jax.random.fold_in(key_list[7], 71), 0),
    }


BETA = 0.95


def reference(grads, piece_position, owner, stat_left, stat_right, root_left, root_right):
    block_count = piece_position.shape[0]
    block_width = grads.shape[1]
    shard_count = N_SHARD
    piece_rows = block_width // shard_count
    slot_count = N_SHARD * N_REPLICA * CAP
    pieces = grads.reshape(shard_count, block_count, piece_rows, block_width)[:, piece_position]
    blocks = jnp.transpose(pieces, (1, 0, 2, 3)).reshape(block_count, block_width, block_width)
    old_left = stat_left.reshape(slot_count, block_width, block_width)
    old_right = stat_right.reshape(slot_count, block_width, block_width)
    slot_left = root_left.reshape(slot_count, block_width, block_width)
    slot_right = root_right.reshape(slot_count, block_width, block_width)

    def precondition(items):
        block, owned = items
        gram_left = jnp.dot(block, block.T, preferred_element_type=jnp.float32)
        gram_right = jnp.dot(block.T, block, preferred_element_type=jnp.float32)
        next_left = BETA * old_left[owned] + (1.0 - BETA) * gram_left
        next_right = BETA * old_right[owned] + (1.0 - BETA) * gram_right
        half = jnp.dot(slot_left[owned], block, preferred_element_type=jnp.float32).astype(jnp.bfloat16)
        direction = jnp.dot(half, slot_right[owned], preferred_element_type=jnp.float32).astype(jnp.bfloat16)
        return next_left, next_right, direction

    next_left, next_right, direction = lax.map(precondition, (blocks, owner))
    new_left = old_left.at[owner].set(next_left).reshape(stat_left.shape)
    new_right = old_right.at[owner].set(next_right).reshape(stat_right.shape)
    dir_pieces = jnp.transpose(direction.reshape(block_count, shard_count, piece_rows, block_width), (1, 0, 2, 3))
    placed = jnp.zeros((shard_count, block_count, piece_rows, block_width), jnp.bfloat16)
    placed = placed.at[:, piece_position].set(dir_pieces)
    return new_left, new_right, placed.reshape(block_count * block_width, block_width)
```

```python
import functools

import jax
import jax.numpy as jnp
from jax import lax
from jax.experimental import pallas as pl
from jax.experimental.pallas import tpu as pltpu
from jax.sharding import PartitionSpec as P

BETA = 0.95
MESH = pl.DeviceIdType.MESH
CORES = 2


def exchange_kernel(
    shards, groups,
    owner, position, grads, root_left, root_right,
    block_out, gathered,
    grads_v, left_v, right_v, outgoing, block, direction,
    load_sem, block_sem, own_sem,
    send1, recv1, send2, recv2, send_sib, recv_sib, send_x, recv_x, send_xs, recv_xs,
):
    me = lax.axis_index("shard")
    group = lax.axis_index("replica")
    chips = groups // CORES
    sibling = group + 1 - 2 * (group % CORES)
    width = grads.shape[2]

    barrier = pltpu.get_barrier_semaphore()
    for k in range(1, shards):
        pl.semaphore_signal(
            barrier, inc=1, device_id={"shard": (me + k) % shards, "replica": group},
            device_id_type=MESH)
    pl.semaphore_signal(
        barrier, inc=1, device_id={"shard": me, "replica": sibling}, device_id_type=MESH)
    for j in range(1, chips):
        pl.semaphore_signal(
            barrier, inc=1,
            device_id={"shard": me, "replica": (group + CORES * j) % groups},
            device_id_type=MESH)

    load_grads = pltpu.make_async_copy(grads, grads_v, load_sem.at[0])
    load_grads.start()
    load_left = pltpu.make_async_copy(root_left, left_v, load_sem.at[1])
    load_left.start()
    load_right = pltpu.make_async_copy(root_right, right_v, load_sem.at[2])
    load_right.start()

    targets = [((me + k) % shards) * groups + group for k in range(shards)]

    def find(b, found):
        o, p = owner[b], position[b]
        return tuple(jnp.where(o == t, p, f) for t, f in zip(targets, found))

    found = lax.fori_loop(0, owner.shape[0], find, (jnp.int32(0),) * shards)

    load_grads.wait()
    for k in range(1, shards):
        outgoing[k] = grads_v[found[k]]
    block[me] = grads_v[found[0]]

    pl.semaphore_wait(barrier, shards - 1 + 1 + chips - 1)

    first = []
    for k in range(1, shards):
        copy = pltpu.make_async_remote_copy(
            src_ref=outgoing.at[k], dst_ref=block.at[me],
            send_sem=send1.at[k], recv_sem=recv1.at[k],
            device_id={"shard": (me + k) % shards, "replica": group}, device_id_type=MESH)
        copy.start()
        first.append(copy)
    load_left.wait()
    load_right.wait()
    for copy in first:
        copy.wait_recv()

    keep = pltpu.make_async_copy(block, block_out, block_sem)
    keep.start()
    whole = block[...].reshape(-1, width)
    half = jnp.dot(left_v[...], whole, preferred_element_type=jnp.float32).astype(jnp.bfloat16)
    direction[...] = jnp.dot(
        half, right_v[...], preferred_element_type=jnp.float32
    ).astype(jnp.bfloat16).reshape(direction.shape)

    pending = []
    second = [None]
    for k in range(1, shards):
        copy = pltpu.make_async_remote_copy(
            src_ref=direction.at[(me + k) % shards], dst_ref=gathered.at[me * groups + group],
            send_sem=send2.at[k], recv_sem=recv2.at[k],
            device_id={"shard": (me + k) % shards, "replica": group}, device_id_type=MESH)
        copy.start()
        second.append(copy)
        pending.append(copy)

    across = [None] * shards
    to_sibling = []

    def forward(k, source, slot):
        across[k] = []
        for j in range(1, chips):
            copy = pltpu.make_async_remote_copy(
                src_ref=source, dst_ref=gathered.at[slot],
                send_sem=send_x.at[k, j], recv_sem=recv_x.at[k, j],
                device_id={"shard": me, "replica": (group + CORES * j) % groups},
                device_id_type=MESH)
            copy.start()
            across[k].append(copy)
            pending.append(copy)
        copy = pltpu.make_async_remote_copy(
            src_ref=source, dst_ref=gathered.at[slot],
            send_sem=send_sib.at[k], recv_sem=recv_sib.at[k],
            device_id={"shard": me, "replica": sibling}, device_id_type=MESH)
        copy.start()
        to_sibling.append(copy)
        pending.append(copy)

    def pass_on(k):
        source_shard = (me + shards - k) % shards
        for j in range(1, chips):
            across[k][j - 1].wait_recv()
            slot = source_shard * groups + (group + groups - CORES * j) % groups
            copy = pltpu.make_async_remote_copy(
                src_ref=gathered.at[slot], dst_ref=gathered.at[slot],
                send_sem=send_xs.at[k, j], recv_sem=recv_xs.at[k, j],
                device_id={"shard": me, "replica": sibling}, device_id_type=MESH)
            copy.start()
            to_sibling.append(copy)
            pending.append(copy)

    forward(0, direction.at[me], me * groups + group)
    own = pltpu.make_async_copy(direction.at[me], gathered.at[me * groups + group], own_sem)
    own.start()
    for k in range(1, shards):
        second[k].wait_recv()
        slot = ((me + shards - k) % shards) * groups + group
        forward(k, gathered.at[slot], slot)
        pass_on(k - 1)
    pass_on(shards - 1)
    for copy in to_sibling:
        copy.wait_recv()
    for copy in first:
        copy.wait_send()
    for copy in pending:
        copy.wait_send()
    own.wait()
    keep.wait()


def update_kernel(
    groups,
    owner, position, gathered, block, stat_left, stat_right,
    new_left, new_right, out,
    block_v, left_v, right_v, load_sem, store_sem, piece_sem,
):
    loads = [
        pltpu.make_async_copy(src, dst, load_sem.at[i])
        for i, (src, dst) in enumerate(
            [(block, block_v), (stat_left, left_v), (stat_right, right_v)])
    ]
    for copy in loads:
        copy.start()
    mine = lax.axis_index("shard") * groups + lax.axis_index("replica")
    count = owner.shape[0]
    moves = [
        pltpu.make_async_copy(gathered.at[owner[b]], out.at[position[b]], piece_sem.at[b])
        for b in range(count)
    ]
    for copy in moves:
        copy.start()
    hits = jnp.int32(0)
    for b in range(count):
        hits = hits + jnp.where(owner[b] == mine, 1, 0)
    occupied = hits > 0
    loads[0].wait()
    loads[1].wait()
    g = block_v[...]
    gram = lax.dot_general(g, g, (((1,), (1,)), ((), ())), preferred_element_type=jnp.float32)
    old = left_v[...]
    left_v[...] = jnp.where(occupied, BETA * old + (1.0 - BETA) * gram, old)
    store_left = pltpu.make_async_copy(left_v, new_left, store_sem.at[0])
    store_left.start()
    loads[2].wait()
    gram = lax.dot_general(g, g, (((0,), (0,)), ((), ())), preferred_element_type=jnp.float32)
    old = right_v[...]
    right_v[...] = jnp.where(occupied, BETA * old + (1.0 - BETA) * gram, old)
    store_right = pltpu.make_async_copy(right_v, new_right, store_sem.at[1])
    store_right.start()
    for copy in moves:
        copy.wait()
    store_left.wait()
    store_right.wait()


def body(shards, groups, grads, piece_position, owner, stat_left, stat_right, root_left, root_right):
    count = piece_position.shape[0]
    width = grads.shape[1]
    rows = grads.shape[0] // count
    chips = groups // CORES
    smem = pl.BlockSpec(memory_space=pltpu.SMEM)
    hbm = pl.BlockSpec(memory_space=pl.ANY)
    dma = pltpu.SemaphoreType.DMA
    square = (width, width)
    pieces = grads.reshape(count, rows, width)
    block, gathered = pl.pallas_call(
        functools.partial(exchange_kernel, shards, groups),
        out_shape=(
            jax.ShapeDtypeStruct((shards, rows, width), jnp.bfloat16),
            jax.ShapeDtypeStruct((shards * groups, rows, width), jnp.bfloat16),
        ),
        in_specs=[smem, smem, hbm, hbm, hbm],
        out_specs=(hbm, hbm),
        scratch_shapes=[
            pltpu.VMEM((count, rows, width), jnp.bfloat16),
            pltpu.VMEM(square, jnp.bfloat16),
            pltpu.VMEM(square, jnp.bfloat16),
            pltpu.VMEM((shards, rows, width), jnp.bfloat16),
            pltpu.VMEM((shards, rows, width), jnp.bfloat16),
            pltpu.VMEM((shards, rows, width), jnp.bfloat16),
            dma((3,)), dma, dma,
            dma((shards,)), dma((shards,)),
            dma((shards,)), dma((shards,)),
            dma((shards,)), dma((shards,)),
            dma((shards, chips)), dma((shards, chips)),
            dma((shards, chips)), dma((shards, chips)),
        ],
        compiler_params=pltpu.CompilerParams(
            collective_id=0, has_side_effects=True, vmem_limit_bytes=40 * 1024 * 1024),
        cost_estimate=pl.CostEstimate(
            flops=4 * width**3, bytes_accessed=8 * width * width * 2, transcendentals=0),
        name="exchange",
    )(owner, piece_position, pieces, root_left.reshape(square), root_right.reshape(square))

    new_left, new_right, out = pl.pallas_call(
        functools.partial(update_kernel, groups),
        out_shape=(
            jax.ShapeDtypeStruct(square, jnp.float32),
            jax.ShapeDtypeStruct(square, jnp.float32),
            jax.ShapeDtypeStruct((count, rows, width), jnp.bfloat16),
        ),
        in_specs=[smem, smem, hbm, hbm, hbm, hbm],
        out_specs=(hbm, hbm, hbm),
        scratch_shapes=[
            pltpu.VMEM(square, jnp.bfloat16),
            pltpu.VMEM(square, jnp.float32),
            pltpu.VMEM(square, jnp.float32),
            dma((3,)), dma((2,)), dma((count,)),
        ],
        compiler_params=pltpu.CompilerParams(vmem_limit_bytes=40 * 1024 * 1024),
        cost_estimate=pl.CostEstimate(
            flops=4 * width**3, bytes_accessed=20 * width * width, transcendentals=0),
        name="update",
    )(owner, piece_position, gathered, block.reshape(square),
      stat_left.reshape(square), stat_right.reshape(square))
    return (
        new_left.reshape(stat_left.shape),
        new_right.reshape(stat_right.shape),
        out.reshape(count * rows, width),
    )


def solution(mesh):
    slots = P("shard", "replica", None, None, None)
    return jax.shard_map(
        functools.partial(body, mesh.shape["shard"], mesh.shape["replica"]),
        mesh=mesh,
        in_specs=(P("shard", None), P(), P(), slots, slots, slots, slots),
        out_specs=(slots, slots, P("shard", None)),
        check_vma=False,
    )
```

```python
import functools

import jax
import jax.numpy as jnp
from jax import lax
from jax.experimental import pallas as pl
from jax.experimental.pallas import tpu as pltpu
from jax.sharding import PartitionSpec as P

BETA = 0.95
MESH = pl.DeviceIdType.MESH
CORES = 2
VMEM_LIMIT = 40 * 1024 * 1024


def partner(me, k, shards):
    if shards & (shards - 1):
        return (shards + k - me) % shards
    bit, other = 1, me
    while bit < shards:
        if k & bit:
            other = other + bit * (1 - 2 * ((me // bit) % 2))
        bit *= 2
    return other


def exchange_kernel(
    shards, groups, order,
    owner, position, grads, root_left, root_right, stat_left, stat_right,
    new_left, new_right, gathered,
    owner_s, position_s, grads_v, left_v, right_v, outgoing, block, direction,
    load_sem, own_sem,
    send1, recv1, send2, recv2, send_sib, recv_sib, send_x, recv_x, send_xs, recv_xs,
):
    me = lax.axis_index("shard")
    group = lax.axis_index("replica")
    chips = groups // CORES
    sibling = group + 1 - 2 * (group % CORES)
    width = grads.shape[2]

    loads = [
        pltpu.make_async_copy(src, dst, load_sem.at[i])
        for i, (src, dst) in enumerate([
            (owner, owner_s), (position, position_s), (grads, grads_v),
            (root_left, left_v), (root_right, right_v),
            (stat_left, new_left), (stat_right, new_right)])
    ]
    for copy in loads[:3]:
        copy.start()

    barrier = pltpu.get_barrier_semaphore()
    for k in order:
        pl.semaphore_signal(
            barrier, inc=1, device_id={"shard": partner(me, k, shards), "replica": group},
            device_id_type=MESH)
    pl.semaphore_signal(
        barrier, inc=1, device_id={"shard": me, "replica": sibling}, device_id_type=MESH)
    for j in range(1, chips):
        pl.semaphore_signal(
            barrier, inc=1,
            device_id={"shard": me, "replica": (group + CORES * j) % groups},
            device_id_type=MESH)
    for copy in loads[3:]:
        copy.start()

    loads[0].wait()
    loads[1].wait()
    mine = me * groups + group
    targets = [((me + k) % shards) * groups + group for k in range(1, shards)]

    def find(b, carry):
        hits, own, found = carry
        o, p = owner_s[b], position_s[b]
        return (
            jnp.where(o == mine, 1, hits),
            jnp.where(o == mine, p, own),
            tuple(jnp.where(o == t, p, f) for t, f in zip(targets, found)),
        )

    zero = jnp.int32(0)
    hits, own, found = lax.fori_loop(
        0, owner.shape[0], find, (zero, zero, (zero,) * (shards - 1)), unroll=4)

    loads[2].wait()
    for k, f in enumerate(found, 1):
        outgoing[k] = grads_v[f]
    block[me] = grads_v[own]

    pl.semaphore_wait(barrier, shards + chips - 1)

    first = []
    for k in range(1, shards):
        copy = pltpu.make_async_remote_copy(
            src_ref=outgoing.at[k], dst_ref=block.at[me],
            send_sem=send1.at[k], recv_sem=recv1.at[k],
            device_id={"shard": (me + k) % shards, "replica": group}, device_id_type=MESH)
        copy.start()
        first.append(copy)
    for copy in loads[3:]:
        copy.wait()
    for copy in first:
        copy.wait_recv()

    whole = block[...].reshape(-1, width)
    half = jnp.dot(left_v[...], whole, preferred_element_type=jnp.float32).astype(jnp.bfloat16)
    direction[...] = jnp.dot(
        half, right_v[...], preferred_element_type=jnp.float32
    ).astype(jnp.bfloat16).reshape(direction.shape)

    pending = []
    second = {}
    across = {}
    to_sibling = []

    def send(source, slot, sends, recvs, shard, replica):
        copy = pltpu.make_async_remote_copy(
            src_ref=source, dst_ref=gathered.at[slot], send_sem=sends, recv_sem=recvs,
            device_id={"shard": shard, "replica": replica}, device_id_type=MESH)
        copy.start()
        pending.append(copy)
        return copy

    def send_across(k, source, slot):
        for j in range(1, chips):
            across[k, j] = send(
                source, slot, send_x.at[k, j], recv_x.at[k, j],
                me, (group + CORES * j) % groups)

    def send_second(k):
        other = partner(me, k, shards)
        second[k] = send(
            direction.at[other], mine, send2.at[k], recv2.at[k], other, group)

    def send_sibling(k, source, slot):
        to_sibling.append(send(source, slot, send_sib.at[k], recv_sib.at[k], me, sibling))

    def arrive(k):
        second[k].wait_recv()
        slot = partner(me, k, shards) * groups + group
        send_across(k, gathered.at[slot], slot)
        send_sibling(k, gathered.at[slot], slot)

    def pass_on(k):
        source_shard = partner(me, k, shards)
        for j in range(1, chips):
            across[k, j].wait_recv()
            slot = source_shard * groups + (group + groups - CORES * j) % groups
            to_sibling.append(send(
                gathered.at[slot], slot, send_xs.at[k, j], recv_xs.at[k, j], me, sibling))

    send_across(0, direction.at[me], mine)
    for k in order:
        send_second(k)
    send_sibling(0, direction.at[me], mine)
    own = pltpu.make_async_copy(direction.at[me], gathered.at[mine], own_sem)
    own.start()

    chunk = width // 4
    occupied = hits > 0
    for i in range(4):
        rows = pl.ds(i * chunk, chunk)
        gram = lax.dot_general(
            whole[i * chunk:(i + 1) * chunk], whole, (((1,), (1,)), ((), ())),
            preferred_element_type=jnp.float32)
        old = new_left[rows]
        new_left[rows] = jnp.where(occupied, BETA * old + (1.0 - BETA) * gram, old)
        gram = lax.dot_general(
            whole[:, i * chunk:(i + 1) * chunk], whole, (((0,), (0,)), ((), ())),
            preferred_element_type=jnp.float32)
        old = new_right[rows]
        new_right[rows] = jnp.where(occupied, BETA * old + (1.0 - BETA) * gram, old)

    last = 0
    for k in order:
        arrive(k)
        pass_on(last)
        last = k
    pass_on(last)
    for copy in to_sibling:
        copy.wait_recv()
    for copy in first:
        copy.wait_send()
    for copy in pending:
        copy.wait_send()
    own.wait()


def place_kernel(
    owner, position, gathered, left, right,
    new_left, new_right, out,
    store_sem, piece_sem,
):
    stores = [
        pltpu.make_async_copy(left, new_left, store_sem.at[0]),
        pltpu.make_async_copy(right, new_right, store_sem.at[1]),
    ]
    for copy in stores:
        copy.start()
    moves = [
        pltpu.make_async_copy(gathered.at[owner[b]], out.at[position[b]], piece_sem.at[b])
        for b in range(owner.shape[0])
    ]
    for copy in moves:
        copy.start()
    for copy in moves + stores:
        copy.wait()


def body(shards, groups, grads, piece_position, owner, stat_left, stat_right, root_left, root_right):
    count = piece_position.shape[0]
    width = grads.shape[1]
    rows = grads.shape[0] // count
    chips = groups // CORES
    order = tuple(range(1, shards))
    smem = pl.BlockSpec(memory_space=pltpu.SMEM)
    hbm = pl.BlockSpec(memory_space=pltpu.HBM)
    anywhere = pl.BlockSpec(memory_space=pl.ANY)
    vmem = pl.BlockSpec(memory_space=pltpu.VMEM)
    dma = pltpu.SemaphoreType.DMA
    square = (width, width)
    pieces = grads.reshape(count, rows, width)
    left, right, gathered = pl.pallas_call(
        functools.partial(exchange_kernel, shards, groups, order),
        out_shape=(
            jax.ShapeDtypeStruct(square, jnp.float32),
            jax.ShapeDtypeStruct(square, jnp.float32),
            jax.ShapeDtypeStruct((shards * groups, rows, width), jnp.bfloat16),
        ),
        in_specs=[hbm] * 7,
        out_specs=(vmem, vmem, anywhere),
        scratch_shapes=[
            pltpu.SMEM((count,), jnp.int32),
            pltpu.SMEM((count,), jnp.int32),
            pltpu.VMEM((count, rows, width), jnp.bfloat16),
            pltpu.VMEM(square, jnp.bfloat16),
            pltpu.VMEM(square, jnp.bfloat16),
            pltpu.VMEM((shards, rows, width), jnp.bfloat16),
            pltpu.VMEM((shards, rows, width), jnp.bfloat16),
            pltpu.VMEM((shards, rows, width), jnp.bfloat16),
            dma((7,)), dma,
            dma((shards,)), dma((shards,)),
            dma((shards,)), dma((shards,)),
            dma((shards,)), dma((shards,)),
            dma((shards, chips)), dma((shards, chips)),
            dma((shards, chips)), dma((shards, chips)),
        ],
        compiler_params=pltpu.CompilerParams(
            collective_id=0, has_side_effects=True, vmem_limit_bytes=VMEM_LIMIT),
        cost_estimate=pl.CostEstimate(
            flops=8 * width**3, bytes_accessed=24 * width * width, transcendentals=0),
        name="exchange",
    )(*[pltpu.with_memory_space_constraint(x, pltpu.HBM) for x in (
        owner, piece_position, pieces, root_left.reshape(square), root_right.reshape(square),
        stat_left.reshape(square), stat_right.reshape(square))])

    new_left, new_right, out = pl.pallas_call(
        place_kernel,
        out_shape=(
            jax.ShapeDtypeStruct(square, jnp.float32),
            jax.ShapeDtypeStruct(square, jnp.float32),
            jax.ShapeDtypeStruct((count, rows, width), jnp.bfloat16),
        ),
        in_specs=[smem, smem, anywhere, anywhere, anywhere],
        out_specs=(hbm, hbm, hbm),
        scratch_shapes=[dma((2,)), dma((count,))],
        compiler_params=pltpu.CompilerParams(vmem_limit_bytes=16 * 1024 * 1024),
        cost_estimate=pl.CostEstimate(
            flops=0, bytes_accessed=16 * width * width, transcendentals=0),
        name="place",
    )(owner, piece_position, gathered, left, right)
    return (
        new_left.reshape(stat_left.shape),
        new_right.reshape(stat_right.shape),
        out.reshape(count * rows, width),
    )


def solution(mesh):
    slots = P("shard", "replica", None, None, None)
    return jax.shard_map(
        functools.partial(body, mesh.shape["shard"], mesh.shape["replica"]),
        mesh=mesh,
        in_specs=(P("shard", None), P(), P(), slots, slots, slots, slots),
        out_specs=(slots, slots, P("shard", None)),
        check_vma=False,
    )
```

```python
import functools

import jax
import jax.numpy as jnp
from jax import lax
from jax.experimental import pallas as pl
from jax.experimental.pallas import tpu as pltpu
from jax.sharding import PartitionSpec as P

BETA = 0.95
MESH = pl.DeviceIdType.MESH
CORES = 2
VMEM_LIMIT = 40 * 1024 * 1024


def partner(me, k, shards):
    if shards & (shards - 1):
        return (shards + k - me) % shards
    bit, other = 1, me
    while bit < shards:
        if k & bit:
            other = other + bit * (1 - 2 * ((me // bit) % 2))
        bit *= 2
    return other


def exchange_kernel(
    shards, groups, order,
    owner, position, grads, root_left, root_right, stat_left, stat_right,
    new_left, new_right, gathered,
    owner_s, position_s, grads_v, left_v, right_v, outgoing, block, direction,
    load_sem, own_sem,
    send1, recv1, send2, recv2, send_sib, recv_sib, send_x, recv_x, send_xs, recv_xs,
):
    me = lax.axis_index("shard")
    group = lax.axis_index("replica")
    chips = groups // CORES
    sibling = group + 1 - 2 * (group % CORES)
    width = grads.shape[2]

    loads = [
        pltpu.make_async_copy(src, dst, load_sem.at[i])
        for i, (src, dst) in enumerate([
            (owner, owner_s), (position, position_s), (grads, grads_v),
            (root_left, left_v), (root_right, right_v),
            (stat_left, new_left), (stat_right, new_right)])
    ]
    for copy in loads[:3]:
        copy.start()

    barrier = pltpu.get_barrier_semaphore()
    for k in order:
        pl.semaphore_signal(
            barrier, inc=1, device_id={"shard": partner(me, k, shards), "replica": group},
            device_id_type=MESH)
    pl.semaphore_signal(
        barrier, inc=1, device_id={"shard": me, "replica": sibling}, device_id_type=MESH)
    for j in range(1, chips):
        pl.semaphore_signal(
            barrier, inc=1,
            device_id={"shard": me, "replica": (group + CORES * j) % groups},
            device_id_type=MESH)
    for copy in loads[3:]:
        copy.start()

    loads[0].wait()
    loads[1].wait()
    mine = me * groups + group
    targets = [((me + k) % shards) * groups + group for k in range(1, shards)]

    def find(b, carry):
        hits, own, found = carry
        o, p = owner_s[b], position_s[b]
        return (
            jnp.where(o == mine, 1, hits),
            jnp.where(o == mine, p, own),
            tuple(jnp.where(o == t, p, f) for t, f in zip(targets, found)),
        )

    zero = jnp.int32(0)
    hits, own, found = lax.fori_loop(
        0, owner.shape[0], find, (zero, zero, (zero,) * (shards - 1)), unroll=4)

    loads[2].wait()
    for k, f in enumerate(found, 1):
        outgoing[k] = grads_v[f]
    block[me] = grads_v[own]

    pl.semaphore_wait(barrier, shards + chips - 1)

    first = []
    for k in range(1, shards):
        copy = pltpu.make_async_remote_copy(
            src_ref=outgoing.at[k], dst_ref=block.at[me],
            send_sem=send1.at[k], recv_sem=recv1.at[k],
            device_id={"shard": (me + k) % shards, "replica": group}, device_id_type=MESH)
        copy.start()
        first.append(copy)
    for copy in loads[3:]:
        copy.wait()
    for copy in first:
        copy.wait_recv()

    whole = block[...].reshape(-1, width)
    half = jnp.dot(left_v[...], whole, preferred_element_type=jnp.float32).astype(jnp.bfloat16)
    direction[...] = jnp.dot(
        half, right_v[...], preferred_element_type=jnp.float32
    ).astype(jnp.bfloat16).reshape(direction.shape)

    pending = []
    second = {}
    across = {}
    to_sibling = []

    def send(source, slot, sends, recvs, shard, replica):
        copy = pltpu.make_async_remote_copy(
            src_ref=source, dst_ref=gathered.at[slot], send_sem=sends, recv_sem=recvs,
            device_id={"shard": shard, "replica": replica}, device_id_type=MESH)
        copy.start()
        pending.append(copy)
        return copy

    def send_across(k, source, slot):
        for j in range(1, chips):
            across[k, j] = send(
                source, slot, send_x.at[k, j], recv_x.at[k, j],
                me, (group + CORES * j) % groups)

    def send_second(k):
        other = partner(me, k, shards)
        second[k] = send(
            direction.at[other], mine, send2.at[k], recv2.at[k], other, group)

    def send_sibling(k, source, slot):
        to_sibling.append(send(source, slot, send_sib.at[k], recv_sib.at[k], me, sibling))

    def arrive(k):
        second[k].wait_recv()
        slot = partner(me, k, shards) * groups + group
        send_across(k, gathered.at[slot], slot)
        send_sibling(k, gathered.at[slot], slot)

    def pass_on(k):
        source_shard = partner(me, k, shards)
        for j in range(1, chips):
            across[k, j].wait_recv()
            slot = source_shard * groups + (group + groups - CORES * j) % groups
            to_sibling.append(send(
                gathered.at[slot], slot, send_xs.at[k, j], recv_xs.at[k, j], me, sibling))

    send_across(0, direction.at[me], mine)
    for k in order[:3]:
        send_second(k)
    send_sibling(0, direction.at[me], mine)
    own = pltpu.make_async_copy(direction.at[me], gathered.at[mine], own_sem)
    own.start()

    chunk = width // 4
    occupied = hits > 0
    for i in range(4):
        rows = pl.ds(i * chunk, chunk)
        gram = lax.dot_general(
            whole[i * chunk:(i + 1) * chunk], whole, (((1,), (1,)), ((), ())),
            preferred_element_type=jnp.float32)
        old = new_left[rows]
        new_left[rows] = jnp.where(occupied, BETA * old + (1.0 - BETA) * gram, old)
        gram = lax.dot_general(
            whole[:, i * chunk:(i + 1) * chunk], whole, (((0,), (0,)), ((), ())),
            preferred_element_type=jnp.float32)
        old = new_right[rows]
        new_right[rows] = jnp.where(occupied, BETA * old + (1.0 - BETA) * gram, old)

    waiting = [0]
    for n, k in enumerate(order):
        if n + 3 < len(order):
            send_second(order[n + 3])
        arrive(k)
        waiting.append(k)
        if len(waiting) > 3:
            pass_on(waiting.pop(0))
    for k in waiting:
        pass_on(k)
    for copy in to_sibling:
        copy.wait_recv()
    for copy in first:
        copy.wait_send()
    for copy in pending:
        copy.wait_send()
    own.wait()


def place_kernel(
    owner, position, gathered, left, right,
    new_left, new_right, out,
    store_sem, piece_sem,
):
    stores = [
        pltpu.make_async_copy(left, new_left, store_sem.at[0]),
        pltpu.make_async_copy(right, new_right, store_sem.at[1]),
    ]
    for copy in stores:
        copy.start()
    moves = [
        pltpu.make_async_copy(gathered.at[owner[b]], out.at[position[b]], piece_sem.at[b])
        for b in range(owner.shape[0])
    ]
    for copy in moves:
        copy.start()
    for copy in moves + stores:
        copy.wait()


def body(shards, groups, grads, piece_position, owner, stat_left, stat_right, root_left, root_right):
    count = piece_position.shape[0]
    width = grads.shape[1]
    rows = grads.shape[0] // count
    chips = groups // CORES
    order = tuple(range(1, shards))
    smem = pl.BlockSpec(memory_space=pltpu.SMEM)
    hbm = pl.BlockSpec(memory_space=pltpu.HBM)
    anywhere = pl.BlockSpec(memory_space=pl.ANY)
    vmem = pl.BlockSpec(memory_space=pltpu.VMEM)
    dma = pltpu.SemaphoreType.DMA
    square = (width, width)
    pieces = grads.reshape(count, rows, width)
    left, right, gathered = pl.pallas_call(
        functools.partial(exchange_kernel, shards, groups, order),
        out_shape=(
            jax.ShapeDtypeStruct(square, jnp.float32),
            jax.ShapeDtypeStruct(square, jnp.float32),
            jax.ShapeDtypeStruct((shards * groups, rows, width), jnp.bfloat16),
        ),
        in_specs=[hbm] * 7,
        out_specs=(vmem, vmem, anywhere),
        scratch_shapes=[
            pltpu.SMEM((count,), jnp.int32),
            pltpu.SMEM((count,), jnp.int32),
            pltpu.VMEM((count, rows, width), jnp.bfloat16),
            pltpu.VMEM(square, jnp.bfloat16),
            pltpu.VMEM(square, jnp.bfloat16),
            pltpu.VMEM((shards, rows, width), jnp.bfloat16),
            pltpu.VMEM((shards, rows, width), jnp.bfloat16),
            pltpu.VMEM((shards, rows, width), jnp.bfloat16),
            dma((7,)), dma,
            dma((shards,)), dma((shards,)),
            dma((shards,)), dma((shards,)),
            dma((shards,)), dma((shards,)),
            dma((shards, chips)), dma((shards, chips)),
            dma((shards, chips)), dma((shards, chips)),
        ],
        compiler_params=pltpu.CompilerParams(
            collective_id=0, has_side_effects=True, vmem_limit_bytes=VMEM_LIMIT),
        cost_estimate=pl.CostEstimate(
            flops=8 * width**3, bytes_accessed=24 * width * width, transcendentals=0),
        name="exchange",
    )(*[pltpu.with_memory_space_constraint(x, pltpu.HBM) for x in (
        owner, piece_position, pieces, root_left.reshape(square), root_right.reshape(square),
        stat_left.reshape(square), stat_right.reshape(square))])

    new_left, new_right, out = pl.pallas_call(
        place_kernel,
        out_shape=(
            jax.ShapeDtypeStruct(square, jnp.float32),
            jax.ShapeDtypeStruct(square, jnp.float32),
            jax.ShapeDtypeStruct((count, rows, width), jnp.bfloat16),
        ),
        in_specs=[smem, smem, anywhere, anywhere, anywhere],
        out_specs=(hbm, hbm, hbm),
        scratch_shapes=[dma((2,)), dma((count,))],
        compiler_params=pltpu.CompilerParams(vmem_limit_bytes=16 * 1024 * 1024),
        cost_estimate=pl.CostEstimate(
            flops=0, bytes_accessed=16 * width * width, transcendentals=0),
        name="place",
    )(owner, piece_position, gathered, left, right)
    return (
        new_left.reshape(stat_left.shape),
        new_right.reshape(stat_right.shape),
        out.reshape(count * rows, width),
    )


def solution(mesh):
    slots = P("shard", "replica", None, None, None)
    return jax.shard_map(
        functools.partial(body, mesh.shape["shard"], mesh.shape["replica"]),
        mesh=mesh,
        in_specs=(P("shard", None), P(), P(), slots, slots, slots, slots),
        out_specs=(slots, slots, P("shard", None)),
        check_vma=False,
    )
```

```python
import functools

import jax
import jax.numpy as jnp
from jax import lax
from jax.experimental import pallas as pl
from jax.experimental.pallas import tpu as pltpu
from jax.sharding import PartitionSpec as P

BETA = 0.95
MESH = pl.DeviceIdType.MESH
CORES = 2
VMEM_LIMIT = 40 * 1024 * 1024


def partner(me, k, shards):
    if shards & (shards - 1):
        return (shards + k - me) % shards
    bit, other = 1, me
    while bit < shards:
        if k & bit:
            other = other + bit * (1 - 2 * ((me // bit) % 2))
        bit *= 2
    return other


def exchange_kernel(
    shards, groups, order,
    owner, position, grads, root_left, root_right, stat_left, stat_right,
    new_left, new_right, gathered,
    owner_s, position_s, grads_v, left_v, right_v, outgoing, block, direction,
    load_sem, fetch_sem, own_sem,
    send1, recv1, send2, recv2, send_sib, recv_sib, send_x, recv_x, send_xs, recv_xs,
):
    me = lax.axis_index("shard")
    group = lax.axis_index("replica")
    chips = groups // CORES
    sibling = group + 1 - 2 * (group % CORES)
    width = grads.shape[2]

    loads = [
        pltpu.make_async_copy(src, dst, load_sem.at[i])
        for i, (src, dst) in enumerate([
            (owner, owner_s), (position, position_s),
            (root_left, left_v), (root_right, right_v),
            (stat_left, new_left), (stat_right, new_right)])
    ]
    quarter = grads.shape[0] // 4
    fetches = [
        pltpu.make_async_copy(
            grads.at[pl.ds(i * quarter, quarter)], grads_v.at[pl.ds(i * quarter, quarter)],
            fetch_sem.at[i])
        for i in range(4)
    ]
    for copy in loads[:2] + fetches:
        copy.start()

    barrier = pltpu.get_barrier_semaphore()
    for k in order:
        pl.semaphore_signal(
            barrier, inc=1, device_id={"shard": partner(me, k, shards), "replica": group},
            device_id_type=MESH)
    pl.semaphore_signal(
        barrier, inc=1, device_id={"shard": me, "replica": sibling}, device_id_type=MESH)
    for j in range(1, chips):
        pl.semaphore_signal(
            barrier, inc=1,
            device_id={"shard": me, "replica": (group + CORES * j) % groups},
            device_id_type=MESH)

    loads[0].wait()
    loads[1].wait()
    mine = me * groups + group
    targets = [((me + k) % shards) * groups + group for k in range(1, shards)]

    def find(b, carry):
        hits, own, found = carry
        o, p = owner_s[b], position_s[b]
        return (
            jnp.where(o == mine, 1, hits),
            jnp.where(o == mine, p, own),
            tuple(jnp.where(o == t, p, f) for t, f in zip(targets, found)),
        )

    zero = jnp.int32(0)
    hits, own, found = lax.fori_loop(
        0, owner.shape[0], find, (zero, zero, (zero,) * (shards - 1)), unroll=4)

    for copy in fetches:
        copy.wait()
    for k, f in enumerate(found, 1):
        outgoing[k] = grads_v[f]
    block[me] = grads_v[own]

    pl.semaphore_wait(barrier, shards + chips - 1)

    first = []
    for k in range(1, shards):
        copy = pltpu.make_async_remote_copy(
            src_ref=outgoing.at[k], dst_ref=block.at[me],
            send_sem=send1.at[k], recv_sem=recv1.at[k],
            device_id={"shard": (me + k) % shards, "replica": group}, device_id_type=MESH)
        copy.start()
        first.append(copy)
    for copy in loads[2:]:
        copy.start()
    for copy in loads[2:]:
        copy.wait()
    for copy in first:
        copy.wait_recv()

    whole = block[...].reshape(-1, width)
    half = jnp.dot(left_v[...], whole, preferred_element_type=jnp.float32).astype(jnp.bfloat16)
    direction[...] = jnp.dot(
        half, right_v[...], preferred_element_type=jnp.float32
    ).astype(jnp.bfloat16).reshape(direction.shape)

    pending = []
    second = {}
    across = {}
    to_sibling = []

    def send(source, slot, sends, recvs, shard, replica):
        copy = pltpu.make_async_remote_copy(
            src_ref=source, dst_ref=gathered.at[slot], send_sem=sends, recv_sem=recvs,
            device_id={"shard": shard, "replica": replica}, device_id_type=MESH)
        copy.start()
        pending.append(copy)
        return copy

    def send_across(k, source, slot):
        for j in range(1, chips):
            across[k, j] = send(
                source, slot, send_x.at[k, j], recv_x.at[k, j],
                me, (group + CORES * j) % groups)

    def send_second(k):
        other = partner(me, k, shards)
        second[k] = send(
            direction.at[other], mine, send2.at[k], recv2.at[k], other, group)

    def send_sibling(k, source, slot):
        to_sibling.append(send(source, slot, send_sib.at[k], recv_sib.at[k], me, sibling))

    def arrive(k):
        second[k].wait_recv()
        slot = partner(me, k, shards) * groups + group
        send_across(k, gathered.at[slot], slot)
        send_sibling(k, gathered.at[slot], slot)

    def pass_on(k):
        source_shard = partner(me, k, shards)
        for j in range(1, chips):
            across[k, j].wait_recv()
            slot = source_shard * groups + (group + groups - CORES * j) % groups
            to_sibling.append(send(
                gathered.at[slot], slot, send_xs.at[k, j], recv_xs.at[k, j], me, sibling))

    send_across(0, direction.at[me], mine)
    for k in order[:3]:
        send_second(k)
    send_sibling(0, direction.at[me], mine)
    own = pltpu.make_async_copy(direction.at[me], gathered.at[mine], own_sem)
    own.start()

    chunk = width // 4
    occupied = hits > 0
    for i in range(4):
        rows = pl.ds(i * chunk, chunk)
        gram = lax.dot_general(
            whole[i * chunk:(i + 1) * chunk], whole, (((1,), (1,)), ((), ())),
            preferred_element_type=jnp.float32)
        old = new_left[rows]
        new_left[rows] = jnp.where(occupied, BETA * old + (1.0 - BETA) * gram, old)
        gram = lax.dot_general(
            whole[:, i * chunk:(i + 1) * chunk], whole, (((0,), (0,)), ((), ())),
            preferred_element_type=jnp.float32)
        old = new_right[rows]
        new_right[rows] = jnp.where(occupied, BETA * old + (1.0 - BETA) * gram, old)

    waiting = [0]
    for n, k in enumerate(order):
        if n + 3 < len(order):
            send_second(order[n + 3])
        arrive(k)
        waiting.append(k)
        if len(waiting) > 3:
            pass_on(waiting.pop(0))
    for k in waiting:
        pass_on(k)
    for copy in to_sibling:
        copy.wait_recv()
    for copy in first:
        copy.wait_send()
    for copy in pending:
        copy.wait_send()
    own.wait()


def place_kernel(
    owner, position, gathered, left, right,
    new_left, new_right, out,
    store_sem, piece_sem,
):
    stores = [
        pltpu.make_async_copy(left, new_left, store_sem.at[0]),
        pltpu.make_async_copy(right, new_right, store_sem.at[1]),
    ]
    for copy in stores:
        copy.start()
    moves = [
        pltpu.make_async_copy(gathered.at[owner[b]], out.at[position[b]], piece_sem.at[b])
        for b in range(owner.shape[0])
    ]
    for copy in moves:
        copy.start()
    for copy in moves + stores:
        copy.wait()


def body(shards, groups, grads, piece_position, owner, stat_left, stat_right, root_left, root_right):
    count = piece_position.shape[0]
    width = grads.shape[1]
    rows = grads.shape[0] // count
    chips = groups // CORES
    order = tuple(range(1, shards))
    smem = pl.BlockSpec(memory_space=pltpu.SMEM)
    hbm = pl.BlockSpec(memory_space=pltpu.HBM)
    anywhere = pl.BlockSpec(memory_space=pl.ANY)
    vmem = pl.BlockSpec(memory_space=pltpu.VMEM)
    dma = pltpu.SemaphoreType.DMA
    square = (width, width)
    pieces = grads.reshape(count, rows, width)
    left, right, gathered = pl.pallas_call(
        functools.partial(exchange_kernel, shards, groups, order),
        out_shape=(
            jax.ShapeDtypeStruct(square, jnp.float32),
            jax.ShapeDtypeStruct(square, jnp.float32),
            jax.ShapeDtypeStruct((shards * groups, rows, width), jnp.bfloat16),
        ),
        in_specs=[hbm] * 7,
        out_specs=(vmem, vmem, anywhere),
        scratch_shapes=[
            pltpu.SMEM((count,), jnp.int32),
            pltpu.SMEM((count,), jnp.int32),
            pltpu.VMEM((count, rows, width), jnp.bfloat16),
            pltpu.VMEM(square, jnp.bfloat16),
            pltpu.VMEM(square, jnp.bfloat16),
            pltpu.VMEM((shards, rows, width), jnp.bfloat16),
            pltpu.VMEM((shards, rows, width), jnp.bfloat16),
            pltpu.VMEM((shards, rows, width), jnp.bfloat16),
            dma((6,)), dma((4,)), dma,
            dma((shards,)), dma((shards,)),
            dma((shards,)), dma((shards,)),
            dma((shards,)), dma((shards,)),
            dma((shards, chips)), dma((shards, chips)),
            dma((shards, chips)), dma((shards, chips)),
        ],
        compiler_params=pltpu.CompilerParams(
            collective_id=0, has_side_effects=True, vmem_limit_bytes=VMEM_LIMIT),
        cost_estimate=pl.CostEstimate(
            flops=8 * width**3, bytes_accessed=24 * width * width, transcendentals=0),
        name="exchange",
    )(*[pltpu.with_memory_space_constraint(x, pltpu.HBM) for x in (
        owner, piece_position, pieces, root_left.reshape(square), root_right.reshape(square),
        stat_left.reshape(square), stat_right.reshape(square))])

    new_left, new_right, out = pl.pallas_call(
        place_kernel,
        out_shape=(
            jax.ShapeDtypeStruct(square, jnp.float32),
            jax.ShapeDtypeStruct(square, jnp.float32),
            jax.ShapeDtypeStruct((count, rows, width), jnp.bfloat16),
        ),
        in_specs=[smem, smem, anywhere, anywhere, anywhere],
        out_specs=(hbm, hbm, hbm),
        scratch_shapes=[dma((2,)), dma((count,))],
        compiler_params=pltpu.CompilerParams(vmem_limit_bytes=16 * 1024 * 1024),
        cost_estimate=pl.CostEstimate(
            flops=0, bytes_accessed=16 * width * width, transcendentals=0),
        name="place",
    )(owner, piece_position, gathered, left, right)
    return (
        new_left.reshape(stat_left.shape),
        new_right.reshape(stat_right.shape),
        out.reshape(count * rows, width),
    )


def solution(mesh):
    slots = P("shard", "replica", None, None, None)
    return jax.shard_map(
        functools.partial(body, mesh.shape["shard"], mesh.shape["replica"]),
        mesh=mesh,
        in_specs=(P("shard", None), P(), P(), slots, slots, slots, slots),
        out_specs=(slots, slots, P("shard", None)),
        check_vma=False,
    )
```
